32 devices in a mesh: dom: 2 (over x), shot: 8 (over z, y), space: 2 (over core).
Axes of the slice: x: 2, y: 2, z: 4, core: 2. Of those that a mesh axis runs over, the one named last changes fastest.
Arguments:
- wave_prev: float32 [16, 64, 64, 128], P(('dom', 'shot'), 'space'), parts along dimension 0, may hold values from -13 to 13
- wave_now: float32 [16, 64, 64, 128], P(('dom', 'shot'), 'space'), parts along dimension 0, may hold values from -13 to 13
- velocity_code: int32 [128, 64, 128], P(('dom', 'space')), parts along dimension 0, may hold values from 0 to 255
- perturb: float32 [128, 64, 128], P(('dom', 'space'), None, 'shot'), parts along dimension 0, may hold values from -3 to 3
- gains: float32 [256, 64], P(('dom', 'shot')), parts along dimension 0, may hold values from 0.25 to 4
- wavelet: float32 [16, 4], P(('dom', 'shot')), parts along dimension 0, may hold values from -12 to 12
- source_index: int32 [16], P(('dom', 'shot')), parts along dimension 0, may hold values from 0 to 524287
- receiver_index: int32 [16, 256], P(('dom', 'shot')), parts along dimension 0, may hold values from 0 to 524287
- absorb_width: int32 [12], P('dom'), parts along dimension 0, may hold values from 4 to 20
Outputs:
- filtered: float32 [128, 64, 128], P(('dom', 'space'), None, 'shot'), parts along dimension 0
- born_field: float32 [16, 64, 64, 128], P(('dom', 'shot'), 'space'), parts along dimension 0
- traces: float32 [16, 2, 256], P(('dom', 'shot')), parts along dimension 0
The draws below stay inside these ranges and needn't reach their ends.
There are 2 independent parts, one for each index of `dom`. The reference program is written for one: setup_inputs(seed, part) draws one part's arguments, and reference() takes and returns one part's arrays. A program takes and returns all parts, laid end to end along the dimension named above; each array names one. Nothing has to cross between parts.
Inputs may be any that keep to these rules, and one draw needn't show every extreme that they name: `absorb_width`: entries are the widths at the low and high end of the first, second and third dimension, in that order. `source_index`: flat row-major cell indices of the whole window. `receiver_index`: flat row-major cell indices of the whole window.
All inputs are finite; a program needn't handle non-finite values.
Results may differ from the reference program's by a relative error of at most 0.0003.
Values sent between devices are 32-bit elements; how exact they have to be, the bound alone decides.
A program may use at most 64 MiB of HBM per device.

```python
import math
import jax
import jax.numpy as jnp

NX = 64
NY = 64
NZ = 128
STEPS_A = 2
STEPS_B = 2
RECV = 256
SHOTS = 8
STEPS = 4


def checkpoint_field(key, salt):
    base = jax.random.fold_in(key, salt)
    scale_key, noise_key = jax.random.split(base, 2)
    scales = jnp.exp(jax.random.uniform(scale_key, (SHOTS, 1, 1, 1), jnp.float32, math.log(0.3), math.log(3.0)))
    field = scales * jnp.clip(jax.random.normal(noise_key, (SHOTS, NX, NY, NZ), jnp.float32), -4.0, 4.0)
    return field.astype(jnp.float32)


def draw_wave_prev(key, part):
    return checkpoint_field(key, 11)


def draw_wave_now(key, part):
    return checkpoint_field(key, 12)


def touch_ends(entries, rng, least, top_value):
    dims = entries.shape
    index_at = [jax.random.randint(jax.random.fold_in(rng, axis), (), 0, dims[axis]) for axis in range(len(dims))]
    entries = entries.at[tuple(index_at)].set(least)
    longest = dims.index(max(dims))
    index_at[longest] = (index_at[longest] + 1) % dims[longest]
    return entries.at[tuple(index_at)].set(top_value)


def block_levels(key, shape, cuts, low, high):
    def one(axis_at, parts):
        heights = jax.random.uniform(jax.random.fold_in(jax.random.fold_in(key, 6), axis_at), (parts,), jnp.float32, low / len(cuts), high / len(cuts))
        return jnp.repeat(jnp.exp(heights), shape[axis_at] // parts).reshape((-1,) + (1,) * (len(shape) - axis_at - 1))

    loudness = one(*cuts[0])
    for cut in cuts[1:]:
        loudness = loudness * one(*cut)
    return loudness


def gaussian(stream_key, shape, deviation, limit, shards=(), kind=jnp.bfloat16):
    result = jax.random.normal(stream_key, shape, jnp.float32) * deviation
    if len(shards) > 0:
        result = block_levels(stream_key, shape, shards, -0.22, 0.18) * result
    return jnp.clip(result, min=-limit, max=limit).astype(kind)


def setup_inputs(seed: int = 0, part: int = 0) -> dict:
    seeds = jax.random.split(jax.random.key(seed), 10)
    own_keys = jax.random.split(jax.random.fold_in(seeds[9], part), 10)
    return {
        "wave_prev": draw_wave_prev(jax.random.fold_in(jax.random.fold_in(seeds[9], part), 71), part),
        "wave_now": draw_wave_now(jax.random.fold_in(jax.random.fold_in(seeds[9], part), 71), part),
        "velocity_code": touch_ends(jax.random.randint(own_keys[2], (NX, NY, NZ), 0, 256), jax.random.fold_in(own_keys[2], 1), 0, 255).astype(jnp.int32),
        "perturb": gaussian(own_keys[3], (NX, NY, NZ), 0.5, 3.0, ((0, 2), (2, 8)), jnp.float32),
        "gains": jnp.clip(jnp.exp(math.log(4.0) - 2.7725887 * jax.random.uniform(own_keys[4], (NZ, NY), jnp.float32) ** block_levels(own_keys[4], (NZ, NY), ((0, 8),), -0.2, 0.2)), 0.25, 4.0),
        "wavelet": gaussian(own_keys[5], (SHOTS, STEPS), 4.0, 12.0, ((0, 8),), jnp.float32),
        "source_index": touch_ends(jax.random.randint(own_keys[6], (SHOTS,), 0, NX * NY * NZ), jax.random.fold_in(own_keys[6], 1), 0, (NX * NY * NZ) - 1).astype(jnp.int32),
        "receiver_index": touch_ends(jax.random.randint(own_keys[7], (SHOTS, RECV), 0, NX * NY * NZ), jax.random.fold_in(own_keys[7], 1), 0, (NX * NY * NZ) - 1).astype(jnp.int32),
        "absorb_width": touch_ends(jax.random.randint(own_keys[8], (6,), 4, NY // 4 + 5), jax.random.fold_in(own_keys[8], 1), 4, (NY // 4 + 5) - 1).astype(jnp.int32),
    }


STENCIL = (-205.0 / 72.0, 8.0 / 5.0, -1.0 / 5.0, 8.0 / 315.0, -1.0 / 560.0)
damp_peak = 0.5
eps = 1e-5


def coefficient(levels):
    speed = 1500.0 + 15.0 * levels.astype(jnp.float32)
    ratio = 0.45 * speed / 5325.0
    return ratio * ratio


def ramp(position, count, lower, upper):
    low_part = jnp.maximum(lower - position, 0.0) / lower
    high_part = jnp.maximum(upper - (count - 1.0 - position), 0.0) / upper
    return low_part * low_part + high_part * high_part


def damping(widths, positions, count_x, count_y, count_z):
    edges = widths.astype(jnp.float32)
    along_x = ramp(positions, count_x, edges[0], edges[1])
    along_y = ramp(jnp.arange(count_y, dtype=jnp.float32), count_y, edges[2], edges[3])
    along_z = ramp(jnp.arange(count_z, dtype=jnp.float32), count_z, edges[4], edges[5])
    return damp_peak * (along_x[:, None, None] + along_y[None, :, None] + along_z[None, None, :])


def widen(field):
    lead = [(0, 0)] * (field.ndim - 3)
    return jnp.pad(field, lead + [(4, 4), (4, 4), (4, 4)])


def laplace(padded):
    width_x = padded.shape[-3] - 8
    width_y = padded.shape[-2] - 8
    width_z = padded.shape[-1] - 8

    def part(move_x, move_y, move_z):
        return padded[..., 4 + move_x:4 + move_x + width_x, 4 + move_y:4 + move_y + width_y, 4 + move_z:4 + move_z + width_z]

    total = 3.0 * STENCIL[0] * part(0, 0, 0)
    for reach in range(1, 5):
        beside_all = part(reach, 0, 0) + part(-reach, 0, 0) + part(0, reach, 0) + part(0, -reach, 0) + part(0, 0, reach) + part(0, 0, -reach)
        total = total + STENCIL[reach] * beside_all
    return total


def reference(wave_prev, wave_now, velocity_code, perturb, gains, wavelet, source_index, receiver_index, absorb_width):
    shots = wave_now.shape[0]
    speed_term = coefficient(velocity_code)
    absorber = damping(absorb_width, jnp.arange(NX, dtype=jnp.float32), NX, NY, NZ)
    term_flat = speed_term.reshape(-1)
    rows = jnp.arange(shots)

    def inject(field, moment):
        flat = field.reshape(shots, -1)
        flat = flat.at[rows, source_index].add(term_flat[source_index] * wavelet[:, moment])
        return flat.reshape(field.shape)

    def advance(current, prior, born, born_prior, model, moment):
        drive = speed_term * laplace(widen(current))
        later = inject(2.0 * current - prior + drive - absorber * (current - prior), moment)
        born_later = 2.0 * born - born_prior + speed_term * laplace(widen(born)) - absorber * (born - born_prior) + model * drive
        return later, born_later, drive

    current, prior = wave_now, wave_prev
    born = jnp.zeros_like(wave_now)
    born_prior = jnp.zeros_like(wave_now)
    image = jnp.zeros((NX, NY, NZ), jnp.float32)
    light = jnp.zeros((NX, NY, NZ), jnp.float32)
    for moment in range(STEPS_A):
        later, born_later, drive = advance(current, prior, born, born_prior, perturb, moment)
        image = image + jnp.sum(drive * born_later, axis=0)
        light = light + jnp.sum(drive * drive, axis=0)
        prior, current = current, later
        born_prior, born = born, born_later
    scaled = image / (light + eps)
    spectrum = jnp.fft.fft(scaled, axis=1) * jnp.transpose(gains)[None, :, :]
    filtered = jnp.real(jnp.fft.ifft(spectrum, axis=1)).astype(jnp.float32)
    born = jnp.zeros_like(wave_now)
    born_prior = jnp.zeros_like(wave_now)
    records = []
    for moment in range(STEPS_B):
        later, born_later, drive = advance(current, prior, born, born_prior, filtered, STEPS_A + moment)
        records.append(jnp.take_along_axis(born_later.reshape(shots, -1), receiver_index, axis=1))
        prior, current = current, later
        born_prior, born = born, born_later
    return filtered, born, jnp.stack(records, axis=1)
```

```python
import math

import jax
import jax.numpy as jnp
import ml_dtypes
import numpy as np
from jax import lax
from jax.experimental import pallas as pl
from jax.experimental.pallas import tpu as pltpu
from jax.sharding import PartitionSpec as P

STEPS_A = 2
STEPS_B = 2


STENCIL = (-205.0 / 72.0, 8.0 / 5.0, -1.0 / 5.0, 8.0 / 315.0, -1.0 / 560.0)
damp_peak = 0.5
eps = 1e-05


def with_halo(x, sides, width):
    for axis, dim in sides:
        size, length = (lax.axis_size(axis), x.shape[dim])
        up = [(i, (i + 1) % size) for i in range(size - 1)]
        down = [(j, i) for i, j in up]
        last = lax.slice_in_dim(x, length - width, length, axis=dim)
        first = lax.slice_in_dim(x, 0, width, axis=dim)
        before = lax.ppermute(last, axis, up)
        after = lax.ppermute(first, axis, down)
        x = jnp.concatenate([before, x, after], axis=dim)
    return x


def coefficient(levels):
    speed = 1500.0 + 15.0 * levels.astype(jnp.float32)
    ratio = 0.45 * speed / 5325.0
    return ratio * ratio


def ramp(position, count, lower, upper):
    low_part = jnp.maximum(lower - position, 0.0) / lower
    high_part = jnp.maximum(upper - (count - 1.0 - position), 0.0) / upper
    return low_part * low_part + high_part * high_part


def damping(widths, positions, count_x, count_y, count_z):
    edges = widths.astype(jnp.float32)
    along_x = ramp(positions, count_x, edges[0], edges[1])
    along_y = ramp(jnp.arange(count_y, dtype=jnp.float32), count_y, edges[2], edges[3])
    along_z = ramp(jnp.arange(count_z, dtype=jnp.float32), count_z, edges[4], edges[5])
    return damp_peak * (along_x[:, None, None] + along_y[None, :, None] + along_z[None, None, :])


def widen(field):
    lead = [(0, 0)] * (field.ndim - 2)
    return jnp.pad(field, lead + [(4, 4), (4, 4)])


def laplace(padded):
    width_x = padded.shape[-3] - 8
    width_y = padded.shape[-2] - 8
    width_z = padded.shape[-1] - 8

    def part(move_x, move_y, move_z):
        return padded[
            ...,
            4 + move_x : 4 + move_x + width_x,
            4 + move_y : 4 + move_y + width_y,
            4 + move_z : 4 + move_z + width_z,
        ]

    total = 3.0 * STENCIL[0] * part(0, 0, 0)
    for reach in range(1, 5):
        beside_all = (
            part(reach, 0, 0)
            + part(-reach, 0, 0)
            + part(0, reach, 0)
            + part(0, -reach, 0)
            + part(0, 0, reach)
            + part(0, 0, -reach)
        )
        total = total + STENCIL[reach] * beside_all
    return total


def lateral_filter(field, table):
    count = field.shape[1]
    index = jnp.arange(count)
    phase = index[:, None] * index[None, :] % count
    angle = 2.0 * math.pi / count * phase.astype(jnp.float32)
    cosine = jnp.cos(angle)
    sine = jnp.sin(angle)
    real_part = jnp.einsum("xyz,yk->xzk", field, cosine, precision=lax.Precision.HIGHEST)
    imag_part = jnp.einsum("xyz,yk->xzk", field, sine, precision=lax.Precision.HIGHEST)
    weight = table[None, :, :]
    back = jnp.einsum("xzk,yk->xyz", real_part * weight, cosine, precision=lax.Precision.HIGHEST)
    back = back + jnp.einsum(
        "xzk,yk->xyz", imag_part * weight, sine, precision=lax.Precision.HIGHEST
    )
    return back / count


def body(
    wave_prev,
    wave_now,
    velocity_code,
    perturb,
    gains,
    wavelet,
    source_index,
    receiver_index,
    absorb_width,
):
    shots, span_x, span_y, span_z = wave_now.shape
    start_x = lax.axis_index("space") * span_x
    total_x = span_x * lax.axis_size("space")
    speed_term = coefficient(velocity_code)
    positions = start_x.astype(jnp.float32) + jnp.arange(span_x, dtype=jnp.float32)
    absorber = damping(absorb_width, positions, total_x, span_y, span_z)
    term_flat = speed_term.reshape(-1)
    cells = span_x * span_y * span_z
    offset = start_x * span_y * span_z
    rows = jnp.arange(shots)
    source_local = source_index - offset
    source_owned = (source_local >= 0) & (source_local < cells)
    source_safe = jnp.clip(source_local, 0, cells - 1)
    source_gain = jnp.where(source_owned, term_flat[source_safe], 0.0)
    model = lax.all_gather(perturb, "shot", axis=2, tiled=True)

    def inject(field, moment):
        flat = field.reshape(shots, -1)
        flat = flat.at[rows, source_safe].add(source_gain * wavelet[:, moment])
        return flat.reshape(field.shape)

    def advance(current, prior, born, field_model, moment, first):
        if first:
            padded = widen(with_halo(current, (("space", 1),), 4))
        else:
            both = widen(with_halo(jnp.stack([current, born]), (("space", 2),), 4))
            padded = both[0]
            born_padded = both[1]
        drive = speed_term * laplace(padded)
        later = inject(2.0 * current - prior + drive - absorber * (current - prior), moment)
        if first:
            born_later = field_model * drive
        else:
            born_later = (
                2.0 * born
                + speed_term * laplace(born_padded)
                - absorber * born
                + field_model * drive
            )
        return (later, born_later, drive)

    current, prior = (wave_now, wave_prev)
    born = None
    image = jnp.zeros((span_x, span_y, span_z), jnp.float32)
    light = jnp.zeros((span_x, span_y, span_z), jnp.float32)
    for moment in range(STEPS_A):
        later, born_later, drive = advance(current, prior, born, model, moment, moment == 0)
        image = image + jnp.sum(drive * born_later, axis=0)
        light = light + jnp.sum(drive * drive, axis=0)
        prior, current = (current, later)
        born = born_later
    planes = gains.shape[0]
    image_all, light_all = lax.psum((image, light), "shot")
    table_all = lax.all_gather(gains, "shot", axis=0, tiled=True)
    new_model = lateral_filter(image_all / (light_all + eps), table_all)
    filtered = lax.dynamic_slice_in_dim(new_model, lax.axis_index("shot") * planes, planes, 2)
    receiver_local = receiver_index - offset
    receiver_owned = (receiver_local >= 0) & (receiver_local < cells)
    receiver_safe = jnp.clip(receiver_local, 0, cells - 1)
    born = None
    records = []
    for moment in range(STEPS_B):
        later, born_later, drive = advance(
            current, prior, born, new_model, STEPS_A + moment, moment == 0
        )
        sample = jnp.take_along_axis(born_later.reshape(shots, -1), receiver_safe, axis=1)
        records.append(jnp.where(receiver_owned, sample, 0.0))
        prior, current = (current, later)
        born = born_later
    traces = lax.psum(jnp.stack(records, axis=1), "space")
    return (filtered, born, traces)


XB = 8
MESH = pl.DeviceIdType.MESH


def swap_groups(tiles, width):
    lane = lax.broadcasted_iota(jnp.int32, tiles[0].shape, 1) // width
    tiles = list(tiles)
    span = width * len(tiles)
    for bit in (1, 2, 4):
        upper = (lane & bit) != 0
        for i in range(len(tiles)):
            if i & bit:
                continue
            a, b = tiles[i], tiles[i | bit]
            tiles[i] = jnp.where(upper, pltpu.roll(b, width * bit, 1), a)
            tiles[i | bit] = jnp.where(upper, b, pltpu.roll(a, span - width * bit, 1))
    return tiles


def window_kernel(
    prev_ref, now_ref, code_ref, pert_ref, gain_ref, cos_ref, band_ref,
    wavelet_ref, source_ref, receiver_ref, width_ref,
    filt_ref, born_ref, trace_ref,
    W, D, B, M, C, A, PAD, BASE, G, LP, LY, LU, LD, IP, IY, IU, ID, H, ROWS, TR,
    in_sem, halo_send, halo_recv, tr_send, tr_recv,
    g_send, g_recv, rs_send, rs_recv,
):
    core = lax.axis_index("space")
    shot = lax.axis_index("shot")
    y = lax.rem(shot, 2)
    z = shot // 2
    nx, ny, nz = code_ref.shape
    width = pert_ref.shape[2]
    groups = nz // width
    start_x = core * nx
    other = {"space": 1 - core}
    beside = {"shot": 2 * z + 1 - y}
    above = {"shot": shot + 2}
    below = {"shot": shot - 2}

    load = pltpu.make_async_copy(now_ref, W.at[0, pl.ds(4, nx), pl.ds(8, ny)], in_sem)
    load.start()

    barrier = pltpu.get_barrier_semaphore()
    pl.semaphore_signal(barrier, inc=1, device_id=other, device_id_type=MESH)
    pl.semaphore_signal(barrier, inc=1, device_id=beside, device_id_type=MESH)

    @pl.when(z < 3)
    def _():
        pl.semaphore_signal(barrier, inc=1, device_id=above, device_id_type=MESH)

    @pl.when(z > 0)
    def _():
        pl.semaphore_signal(barrier, inc=1, device_id=below, device_id_type=MESH)

    lane_group = lax.broadcasted_iota(jnp.int32, (8, nz), 1) // width

    @pl.loop(0, nx)
    def _(i):
        PAD[:, 0:width] = pert_ref[i]
        tile = PAD[0:8, :]
        for g in range(1, groups):
            tile = jnp.where(lane_group == g, pltpu.roll(PAD[8 * g : 8 * g + 8, :], width * g, 1), tile)
        G[0, shot, i] = tile

    @pl.when((z > 0) & (z < 3))
    def _():
        pl.semaphore_wait(barrier, 4)

    @pl.when((z == 0) | (z == 3))
    def _():
        pl.semaphore_wait(barrier, 3)

    def copy(src, dst, send, recv, device):
        return pltpu.make_async_remote_copy(
            src_ref=src, dst_ref=dst, send_sem=send, recv_sem=recv, device_id=device, device_id_type=MESH
        )

    def gather_copy(n, way, at, device):
        slot = 2 * at + y
        return copy(G.at[n, slot], G.at[n, slot], g_send.at[n, way, at], g_recv.at[n, slot], device)

    def gather_wait(n, slot):
        copy(G.at[n, slot], G.at[n, slot], g_send.at[n, 0, 0], g_recv.at[n, slot], beside).wait_recv()

    def gather_start(n):
        @pl.when(z < 3)
        def _():
            gather_copy(n, 1, z, above).start()

        @pl.when(z > 0)
        def _():
            gather_copy(n, 2, z, below).start()

        gather_copy(n, 0, z, beside).start()

    def gather_forward(n, d):
        @pl.when(z - d >= 0)
        def _():
            gather_wait(n, 2 * (z - d) + y)

            @pl.when(z < 3)
            def _():
                gather_copy(n, 1, z - d, above).start()

            gather_copy(n, 0, z - d, beside).start()

        @pl.when(z + d <= 3)
        def _():
            gather_wait(n, 2 * (z + d) + y)

            @pl.when(z > 0)
            def _():
                gather_copy(n, 2, z + d, below).start()

            gather_copy(n, 0, z + d, beside).start()

    def gather_end(n):
        for at in range(4):
            gather_wait(n, 2 * at + 1 - y)

    def gather_drain(n):
        for at in range(4):
            gather_copy(n, 0, at, beside).wait_send()

            @pl.when((z < 3) & (at <= z))
            def _():
                gather_copy(n, 1, at, above).wait_send()

            @pl.when((z > 0) & (at >= z))
            def _():
                gather_copy(n, 2, at, below).wait_send()

    sums = ((LP, LY, LU, LD), (IP, IY, IU, ID))

    def pair_copy(n, at):
        P_, Y_, _, _ = sums[n]
        return copy(P_.at[2 * at + 1 - y], Y_.at[at], rs_send.at[n, 0, at], rs_recv.at[n, 0, at], beside)

    def up_copy(n, at):
        P_, _, U_, _ = sums[n]
        return copy(P_.at[2 * at + y], U_.at[at], rs_send.at[n, 1, at], rs_recv.at[n, 1, at], above)

    def down_copy(n, at):
        P_, _, _, D_ = sums[n]
        return copy(P_.at[2 * at + y], D_.at[at], rs_send.at[n, 2, at], rs_recv.at[n, 2, at], below)

    def pair_start(n):
        for d in (3, 2, 1):
            @pl.when(z + d <= 3)
            def _():
                pair_copy(n, z + d).start()

            @pl.when(z - d >= 0)
            def _():
                pair_copy(n, z - d).start()

        pair_copy(n, z).start()

    def sum_line(n):
        P_, Y_, U_, D_ = sums[n]
        for d in (3, 2, 1):
            @pl.when(z + d <= 3)
            def _():
                at = z + d
                pair_copy(n, at).wait_recv()
                P_[2 * at + y] = P_[2 * at + y] + Y_[at]

                @pl.when(z > 0)
                def _():
                    up_copy(n, at).wait_recv()
                    P_[2 * at + y] = P_[2 * at + y] + U_[at]

                up_copy(n, at).start()

            @pl.when(z - d >= 0)
            def _():
                at = z - d
                pair_copy(n, at).wait_recv()
                P_[2 * at + y] = P_[2 * at + y] + Y_[at]

                @pl.when(z < 3)
                def _():
                    down_copy(n, at).wait_recv()
                    P_[2 * at + y] = P_[2 * at + y] + D_[at]

                down_copy(n, at).start()

    def sum_own(n):
        P_, Y_, U_, D_ = sums[n]
        pair_copy(n, z).wait_recv()
        P_[shot] = P_[shot] + Y_[z]

        @pl.when(z > 0)
        def _():
            up_copy(n, z).wait_recv()
            P_[shot] = P_[shot] + U_[z]

        @pl.when(z < 3)
        def _():
            down_copy(n, z).wait_recv()
            P_[shot] = P_[shot] + D_[z]

    def sum_drain(n):
        for at in range(4):
            pair_copy(n, at).wait_send()

            @pl.when(at > z)
            def _():
                up_copy(n, at).wait_send()

            @pl.when(at < z)
            def _():
                down_copy(n, at).wait_send()

    fields = [W.at[0], W.at[1], W.at[2], W.at[3], B.at[0], B.at[1]]

    def halo(n):
        field = fields[n]
        return copy(
            field.at[pl.ds(4 + (nx - 4) * (1 - core), 4), pl.ds(8, ny)],
            field.at[pl.ds((nx + 4) * core, 4), pl.ds(8, ny)],
            halo_send.at[n],
            halo_recv.at[n],
            other,
        )

    gather_start(0)
    load.wait()
    halo(0).start()

    edges = [jnp.full((ny, nz), width_ref[i].astype(jnp.float32)) for i in range(6)]

    def ramp_at(position, count, lower, upper):
        low_part = jnp.maximum(lower - position, 0.0) / lower
        high_part = jnp.maximum(upper - (count - 1.0 - position), 0.0) / upper
        return low_part * low_part + high_part * high_part

    row = lax.broadcasted_iota(jnp.int32, (ny, nz), 0)
    column = lax.broadcasted_iota(jnp.int32, (ny, nz), 1)
    flat = row * nz + column
    BASE[...] = damp_peak * (
        ramp_at(row.astype(jnp.float32), ny, edges[2], edges[3])
        + ramp_at(column.astype(jnp.float32), nz, edges[4], edges[5])
    )

    @pl.loop(0, nx)
    def _(i):
        C[i] = coefficient(code_ref[i])
        position = jnp.full((8, nz), (start_x + i).astype(jnp.float32))
        along = ramp_at(position, 2 * nx, edges[0][0:8], edges[1][0:8])
        A[i] = BASE[...] + damp_peak * jnp.concatenate([along] * (ny // 8), axis=0)

    nothing = jnp.zeros((nx, 8, nz), jnp.float32)
    for n in range(6):
        fields[n][pl.ds(4, nx), 0:8, :] = nothing
        fields[n][pl.ds(4, nx), ny + 8 : ny + 16, :] = nothing
        fields[n][pl.ds((nx + 4) * core, 4), 8 : ny + 8, :] = jnp.zeros((4, ny, nz), jnp.float32)

    def along_z(field, i):
        v = field[pl.ds(i + 4, XB), 8 : ny + 8, :].reshape(XB * ny, nz)
        high = v.astype(jnp.bfloat16)
        low = (v - high.astype(jnp.float32)).astype(jnp.bfloat16)
        both = jnp.dot(jnp.concatenate([high, low], axis=1), band_ref[...], preferred_element_type=jnp.float32)
        return both[:, :nz] + both[:, nz:]

    def plane_laplace(field, j, part):
        v = field[j + 4, 8 : ny + 8, :]
        total = 3.0 * STENCIL[0] * v + part
        for k in range(1, 5):
            total = total + STENCIL[k] * (
                (field[j + 4 + k, 8 : ny + 8, :] + field[j + 4 - k, 8 : ny + 8, :])
                + (field[j + 4, 8 + k : ny + 8 + k, :] + field[j + 4, 8 - k : ny + 8 - k, :])
            )
        return v, total

    source = source_ref[0] - start_x * ny * nz

    def wave_step(m):
        halo(m).wait_recv()
        amplitude = wavelet_ref[0, m]

        @pl.loop(0, nx // XB)
        def _(t):
            part = along_z(fields[m], t * XB)
            for p in range(XB):
                j = t * XB + p
                v, total = plane_laplace(fields[m], j, part[p * ny : (p + 1) * ny])
                drive = C[j] * total
                D[m, j] = drive
                if m < 3:
                    prior = prev_ref[j] if m == 0 else fields[m - 1][j + 4, 8 : ny + 8, :]
                    change = v - prior
                    later = v + change + drive - A[j] * change
                    here = flat == source - j * (ny * nz)
                    later = later + jnp.where(here, C[j] * amplitude, 0.0)
                    fields[m + 1][j + 4, 8 : ny + 8, :] = later

        if m < 3:
            halo(m + 1).start()

    def pack(dest, i, value):
        tiles = swap_groups([value[8 * g : 8 * g + 8] for g in range(groups)], width)
        for g in range(groups):
            dest[g, i] = tiles[g]

    def unpack(n, born, drive):
        @pl.loop(0, nx)
        def _(i):
            tiles = swap_groups([G[n, g, i] for g in range(groups)], width)
            model = jnp.concatenate(tiles, axis=0)
            M[i] = model
            fields[born][i + 4, 8 : ny + 8, :] = model * D[drive, i]

        halo(born).start()

    def born_step(born, drive, finish):
        @pl.loop(0, nx // XB)
        def _(t):
            part = along_z(fields[born], t * XB)
            for p in range(XB):
                j = t * XB + p
                v, total = plane_laplace(fields[born], j, part[p * ny : (p + 1) * ny])
                later = 2.0 * v + C[j] * total - A[j] * v + M[j] * D[drive, j]
                finish(j, v, later)

    wave_step(0)
    gather_forward(0, 1)
    wave_step(1)
    gather_forward(0, 2)

    @pl.loop(0, nx)
    def _(i):
        pack(LP, i, D[0, i] * D[0, i] + D[1, i] * D[1, i])

    gather_forward(0, 3)
    pair_start(0)
    H[...] = jnp.dot(
        cos_ref[...], gain_ref[...], precision=lax.Precision.HIGHEST, preferred_element_type=jnp.float32
    )
    gather_end(0)
    unpack(0, 4, 0)
    halo(4).wait_recv()

    def finish_image(j, v, later):
        pack(IP, j, D[0, j] * v + D[1, j] * later)

    born_step(4, 1, finish_image)
    pair_start(1)
    wave_step(2)
    sum_line(0)
    wave_step(3)
    sum_line(1)
    sum_own(0)
    sum_own(1)

    sub = lax.broadcasted_iota(jnp.int32, (8, nz), 0)

    @pl.loop(0, nx // 2)
    def _(t):
        for p in range(2):
            i = 2 * t + p
            scaled = IP[shot, i] / (LP[shot, i] + eps)
            moved = [scaled]
            for q in range(1, 8):
                turned = pltpu.roll(scaled, q, 0)
                moved.append(jnp.where(sub < q, pltpu.roll(turned, width, 1), turned))
            result = None
            for g in range(groups):
                term = moved[0] * H[8 * g : 8 * g + 1, :]
                for q in range(1, 8):
                    term = term + moved[q] * H[8 * g + q : 8 * g + q + 1, :]
                if g:
                    result = result + pltpu.roll(term, width * g, 1)
                else:
                    result = term
            G[1, shot, i] = result

    gather_start(1)

    @pl.loop(0, nx)
    def _(i):
        tile = G[1, shot, i]
        filt_ref[i, 0:8, :] = tile[:, 0:width]
        for g in range(1, groups):
            filt_ref[i, 8 * g : 8 * g + 8, :] = pltpu.roll(tile, nz - width * g, 1)[:, 0:width]

    for d in (1, 2, 3):
        gather_forward(1, d)
    gather_end(1)
    unpack(1, 5, 2)

    count = receiver_ref.shape[1]
    lanes = lax.broadcasted_iota(jnp.int32, (1, nz), 1)
    ones = jnp.ones((8, nz), jnp.float32)

    def record(m, read):
        @pl.loop(0, count // 8)
        def _(t):
            for p in range(8):
                r = t * 8 + p
                local = receiver_ref[0, r] - start_x * ny * nz
                owned = (local >= 0) & (local < nx * ny * nz)
                safe = jnp.clip(local, 0, nx * ny * nz - 1)
                at = jnp.where(owned, safe & (nz - 1), -1)
                line = read(safe // (ny * nz), (safe // nz) & (ny - 1))
                ROWS[pl.ds(r, 1), :] = jnp.where(lanes == at, line, 0.0)

        TR[0, m] = lax.dot_general(
            ones, ROWS[...], (((1,), (1,)), ((), ())),
            precision=lax.Precision.HIGHEST, preferred_element_type=jnp.float32,
        )

    halo(5).wait_recv()
    record(0, lambda px, py: B[1, px + 4, pl.ds(py + 8, 1), :])

    def finish_born(j, v, later):
        born_ref[j] = later

    born_step(5, 3, finish_born)
    record(1, lambda px, py: born_ref[px, pl.ds(py, 1), :])
    swap = copy(TR.at[0], TR.at[1], tr_send, tr_recv, other)
    swap.start()
    for n in range(2):
        gather_drain(n)
        sum_drain(n)
    for n in range(6):
        halo(n).wait_send()
    swap.wait()
    for m in range(2):
        trace_ref[m : m + 1, :] = TR[0, m, 0:1, :] + TR[1, m, 0:1, :]


def fast_body(
    wave_prev, wave_now, velocity_code, perturb, gains, wavelet, source_index, receiver_index, absorb_width
):
    shape = wave_now.shape[1:]
    nx, ny, nz = shape
    planes, receivers = gains.shape[0], receiver_index.shape[1]
    groups = nz // planes
    index = np.arange(ny)
    cosine = (np.cos(2.0 * np.pi / ny * (index[:, None] * index[None, :] % ny)) / ny).astype(np.float32)
    band = np.zeros((nz, nz), np.float32)
    for k in range(1, 5):
        band += STENCIL[k] * (np.eye(nz, k=k) + np.eye(nz, k=-k)).astype(np.float32)
    high = band.astype(ml_dtypes.bfloat16)
    low = (band - high.astype(np.float32)).astype(ml_dtypes.bfloat16)
    band = np.concatenate([np.concatenate([high, low], 1)] * 2, 0)
    tiled = jnp.tile(gains.T, (1, groups))
    block = (nx, 8, nz)
    f32 = jnp.float32
    vmem = pl.BlockSpec(memory_space=pltpu.VMEM)
    smem = pl.BlockSpec(memory_space=pltpu.SMEM)
    v = lambda *dims: pltpu.VMEM(dims, f32)
    dma = pltpu.SemaphoreType.DMA
    filtered, born, traces = pl.pallas_call(
        window_kernel,
        out_shape=(
            jax.ShapeDtypeStruct((nx, ny, planes), f32),
            jax.ShapeDtypeStruct(shape, f32),
            jax.ShapeDtypeStruct((STEPS_B, receivers), f32),
        ),
        in_specs=[vmem, pl.BlockSpec(memory_space=pl.ANY)] + [vmem] * 5 + [smem] * 4,
        out_specs=(vmem, vmem, vmem),
        scratch_shapes=[
            v(4, nx + 8, ny + 16, nz),
            v(4, *shape),
            v(2, nx + 8, ny + 16, nz),
            v(*shape),
            v(*shape),
            v(*shape),
            v(ny, nz),
            v(ny, nz),
            v(2, groups, *block),
        ]
        + [v(groups, *block), v(4, *block), v(4, *block), v(4, *block)] * 2
        + [
            v(ny, nz),
            v(receivers, nz),
            v(2, STEPS_B, 8, receivers),
            dma,
            dma((6,)),
            dma((6,)),
            dma,
            dma,
            dma((2, 3, 4)),
            dma((2, groups)),
            dma((2, 3, 4)),
            dma((2, 3, 4)),
        ],
        compiler_params=pltpu.CompilerParams(
            collective_id=0, has_side_effects=True, vmem_limit_bytes=48 * 1024 * 1024
        ),
    )(
        wave_prev.reshape(shape), wave_now.reshape(shape), velocity_code, perturb, tiled, cosine, band,
        wavelet, source_index, receiver_index, absorb_width,
    )
    return filtered, born[None], traces[None]


def choose(*args):
    wave_now, gains = args[1], args[4]
    shots, _, span_y, span_z = wave_now.shape
    size = lax.axis_size("shot")
    fits = shots == 1 and size == 8 and lax.axis_size("space") == 2
    if fits and span_y == 64 and span_z == 128 and gains.shape[0] == 16:
        return fast_body(*args)
    return body(*args)


def solution(mesh):
    in_specs = (
        P(("dom", "shot"), "space", None, None),
        P(("dom", "shot"), "space", None, None),
        P(("dom", "space"), None, None),
        P(("dom", "space"), None, "shot"),
        P(("dom", "shot"), None),
        P(("dom", "shot"), None),
        P(("dom", "shot")),
        P(("dom", "shot"), None),
        P("dom"),
    )
    out_specs = (
        P(("dom", "space"), None, "shot"),
        P(("dom", "shot"), "space", None, None),
        P(("dom", "shot"), None, None),
    )
    return jax.shard_map(choose, mesh=mesh, in_specs=in_specs, out_specs=out_specs, check_vma=False)
```

```python
import math

import jax
import jax.numpy as jnp
import ml_dtypes
import numpy as np
from jax import lax
from jax.experimental import pallas as pl
from jax.experimental.pallas import tpu as pltpu
from jax.sharding import PartitionSpec as P

STEPS_A = 2
STEPS_B = 2


STENCIL = (-205.0 / 72.0, 8.0 / 5.0, -1.0 / 5.0, 8.0 / 315.0, -1.0 / 560.0)
damp_peak = 0.5
eps = 1e-05


def with_halo(x, sides, width):
    for axis, dim in sides:
        size, length = (lax.axis_size(axis), x.shape[dim])
        up = [(i, (i + 1) % size) for i in range(size - 1)]
        down = [(j, i) for i, j in up]
        last = lax.slice_in_dim(x, length - width, length, axis=dim)
        first = lax.slice_in_dim(x, 0, width, axis=dim)
        before = lax.ppermute(last, axis, up)
        after = lax.ppermute(first, axis, down)
        x = jnp.concatenate([before, x, after], axis=dim)
    return x


def coefficient(levels):
    speed = 1500.0 + 15.0 * levels.astype(jnp.float32)
    ratio = 0.45 * speed / 5325.0
    return ratio * ratio


def ramp(position, count, lower, upper):
    low_part = jnp.maximum(lower - position, 0.0) / lower
    high_part = jnp.maximum(upper - (count - 1.0 - position), 0.0) / upper
    return low_part * low_part + high_part * high_part


def damping(widths, positions, count_x, count_y, count_z):
    edges = widths.astype(jnp.float32)
    along_x = ramp(positions, count_x, edges[0], edges[1])
    along_y = ramp(jnp.arange(count_y, dtype=jnp.float32), count_y, edges[2], edges[3])
    along_z = ramp(jnp.arange(count_z, dtype=jnp.float32), count_z, edges[4], edges[5])
    return damp_peak * (along_x[:, None, None] + along_y[None, :, None] + along_z[None, None, :])


def widen(field):
    lead = [(0, 0)] * (field.ndim - 2)
    return jnp.pad(field, lead + [(4, 4), (4, 4)])


def laplace(padded):
    width_x = padded.shape[-3] - 8
    width_y = padded.shape[-2] - 8
    width_z = padded.shape[-1] - 8

    def part(move_x, move_y, move_z):
        return padded[
            ...,
            4 + move_x : 4 + move_x + width_x,
            4 + move_y : 4 + move_y + width_y,
            4 + move_z : 4 + move_z + width_z,
        ]

    total = 3.0 * STENCIL[0] * part(0, 0, 0)
    for reach in range(1, 5):
        beside_all = (
            part(reach, 0, 0)
            + part(-reach, 0, 0)
            + part(0, reach, 0)
            + part(0, -reach, 0)
            + part(0, 0, reach)
            + part(0, 0, -reach)
        )
        total = total + STENCIL[reach] * beside_all
    return total


def lateral_filter(field, table):
    count = field.shape[1]
    index = jnp.arange(count)
    phase = index[:, None] * index[None, :] % count
    angle = 2.0 * math.pi / count * phase.astype(jnp.float32)
    cosine = jnp.cos(angle)
    sine = jnp.sin(angle)
    real_part = jnp.einsum("xyz,yk->xzk", field, cosine, precision=lax.Precision.HIGHEST)
    imag_part = jnp.einsum("xyz,yk->xzk", field, sine, precision=lax.Precision.HIGHEST)
    weight = table[None, :, :]
    back = jnp.einsum("xzk,yk->xyz", real_part * weight, cosine, precision=lax.Precision.HIGHEST)
    back = back + jnp.einsum(
        "xzk,yk->xyz", imag_part * weight, sine, precision=lax.Precision.HIGHEST
    )
    return back / count


def body(
    wave_prev,
    wave_now,
    velocity_code,
    perturb,
    gains,
    wavelet,
    source_index,
    receiver_index,
    absorb_width,
):
    shots, span_x, span_y, span_z = wave_now.shape
    start_x = lax.axis_index("space") * span_x
    total_x = span_x * lax.axis_size("space")
    speed_term = coefficient(velocity_code)
    positions = start_x.astype(jnp.float32) + jnp.arange(span_x, dtype=jnp.float32)
    absorber = damping(absorb_width, positions, total_x, span_y, span_z)
    term_flat = speed_term.reshape(-1)
    cells = span_x * span_y * span_z
    offset = start_x * span_y * span_z
    rows = jnp.arange(shots)
    source_local = source_index - offset
    source_owned = (source_local >= 0) & (source_local < cells)
    source_safe = jnp.clip(source_local, 0, cells - 1)
    source_gain = jnp.where(source_owned, term_flat[source_safe], 0.0)
    model = lax.all_gather(perturb, "shot", axis=2, tiled=True)

    def inject(field, moment):
        flat = field.reshape(shots, -1)
        flat = flat.at[rows, source_safe].add(source_gain * wavelet[:, moment])
        return flat.reshape(field.shape)

    def advance(current, prior, born, field_model, moment, first):
        if first:
            padded = widen(with_halo(current, (("space", 1),), 4))
        else:
            both = widen(with_halo(jnp.stack([current, born]), (("space", 2),), 4))
            padded = both[0]
            born_padded = both[1]
        drive = speed_term * laplace(padded)
        later = inject(2.0 * current - prior + drive - absorber * (current - prior), moment)
        if first:
            born_later = field_model * drive
        else:
            born_later = (
                2.0 * born
                + speed_term * laplace(born_padded)
                - absorber * born
                + field_model * drive
            )
        return (later, born_later, drive)

    current, prior = (wave_now, wave_prev)
    born = None
    image = jnp.zeros((span_x, span_y, span_z), jnp.float32)
    light = jnp.zeros((span_x, span_y, span_z), jnp.float32)
    for moment in range(STEPS_A):
        later, born_later, drive = advance(current, prior, born, model, moment, moment == 0)
        image = image + jnp.sum(drive * born_later, axis=0)
        light = light + jnp.sum(drive * drive, axis=0)
        prior, current = (current, later)
        born = born_later
    planes = gains.shape[0]
    image_all, light_all = lax.psum((image, light), "shot")
    table_all = lax.all_gather(gains, "shot", axis=0, tiled=True)
    new_model = lateral_filter(image_all / (light_all + eps), table_all)
    filtered = lax.dynamic_slice_in_dim(new_model, lax.axis_index("shot") * planes, planes, 2)
    receiver_local = receiver_index - offset
    receiver_owned = (receiver_local >= 0) & (receiver_local < cells)
    receiver_safe = jnp.clip(receiver_local, 0, cells - 1)
    born = None
    records = []
    for moment in range(STEPS_B):
        later, born_later, drive = advance(
            current, prior, born, new_model, STEPS_A + moment, moment == 0
        )
        sample = jnp.take_along_axis(born_later.reshape(shots, -1), receiver_safe, axis=1)
        records.append(jnp.where(receiver_owned, sample, 0.0))
        prior, current = (current, later)
        born = born_later
    traces = lax.psum(jnp.stack(records, axis=1), "space")
    return (filtered, born, traces)


XB = 8
MESH = pl.DeviceIdType.MESH


def swap_groups(tiles, width):
    lane = lax.broadcasted_iota(jnp.int32, tiles[0].shape, 1) // width
    tiles = list(tiles)
    span = width * len(tiles)
    for bit in (1, 2, 4):
        upper = (lane & bit) != 0
        for i in range(len(tiles)):
            if i & bit:
                continue
            a, b = tiles[i], tiles[i | bit]
            tiles[i] = jnp.where(upper, pltpu.roll(b, width * bit, 1), a)
            tiles[i | bit] = jnp.where(upper, b, pltpu.roll(a, span - width * bit, 1))
    return tiles


def window_kernel(
    prev_ref, now_ref, code_ref, pert_ref, gain_ref, cos_ref, band_ref,
    wavelet_ref, source_ref, receiver_ref, width_ref,
    filt_ref, born_ref, trace_ref,
    W, D, B, M, C, A, CODE, PREV, BASE, G, LP, LY, LU, LD, IP, IY, IU, ID, H, ROWS, TR,
    in_sem, code_sem, prev_sem, halo_send, halo_recv, tr_send, tr_recv,
    g_send, g_recv, rs_send, rs_recv,
):
    core = lax.axis_index("space")
    shot = lax.axis_index("shot")
    y = lax.rem(shot, 2)
    z = shot // 2
    nx, ny, nz = C.shape
    width = pert_ref.shape[1]
    groups = nz // width
    start_x = core * nx
    other = {"space": 1 - core}
    beside = {"shot": 2 * z + 1 - y}
    above = {"shot": shot + 2}
    below = {"shot": shot - 2}

    load = pltpu.make_async_copy(now_ref, W.at[0, pl.ds(4, nx), pl.ds(8, ny)], in_sem)
    load.start()
    load_code = pltpu.make_async_copy(code_ref, CODE, code_sem)
    load_code.start()
    load_prev = pltpu.make_async_copy(prev_ref, PREV, prev_sem)
    load_prev.start()

    barrier = pltpu.get_barrier_semaphore()
    pl.semaphore_signal(barrier, inc=1, device_id=other, device_id_type=MESH)
    pl.semaphore_signal(barrier, inc=1, device_id=beside, device_id_type=MESH)

    @pl.when(z < 3)
    def _():
        pl.semaphore_signal(barrier, inc=1, device_id=above, device_id_type=MESH)

    @pl.when(z > 0)
    def _():
        pl.semaphore_signal(barrier, inc=1, device_id=below, device_id_type=MESH)

    for t in range(nx // groups):
        turned = pert_ref[groups * t : groups * t + groups].reshape(nz, ny).T
        tiles = swap_groups([turned[8 * g : 8 * g + 8] for g in range(groups)], width)
        for g in range(groups):
            G[0, shot, groups * t + g] = tiles[g]

    @pl.when((z > 0) & (z < 3))
    def _():
        pl.semaphore_wait(barrier, 4)

    @pl.when((z == 0) | (z == 3))
    def _():
        pl.semaphore_wait(barrier, 3)

    def copy(src, dst, send, recv, device):
        return pltpu.make_async_remote_copy(
            src_ref=src, dst_ref=dst, send_sem=send, recv_sem=recv, device_id=device, device_id_type=MESH
        )

    def gather_copy(n, way, at, device):
        slot = 2 * at + y
        return copy(G.at[n, slot], G.at[n, slot], g_send.at[n, way, at], g_recv.at[n, slot], device)

    def gather_wait(n, slot):
        copy(G.at[n, slot], G.at[n, slot], g_send.at[n, 0, 0], g_recv.at[n, slot], beside).wait_recv()

    def gather_start(n):
        @pl.when(z < 3)
        def _():
            gather_copy(n, 1, z, above).start()

        @pl.when(z > 0)
        def _():
            gather_copy(n, 2, z, below).start()

        gather_copy(n, 0, z, beside).start()

    def gather_forward(n, d):
        @pl.when(z - d >= 0)
        def _():
            gather_wait(n, 2 * (z - d) + y)

            @pl.when(z < 3)
            def _():
                gather_copy(n, 1, z - d, above).start()

            gather_copy(n, 0, z - d, beside).start()

        @pl.when(z + d <= 3)
        def _():
            gather_wait(n, 2 * (z + d) + y)

            @pl.when(z > 0)
            def _():
                gather_copy(n, 2, z + d, below).start()

            gather_copy(n, 0, z + d, beside).start()

    def gather_end(n):
        for at in range(4):
            gather_wait(n, 2 * at + 1 - y)

    def gather_drain(n):
        for at in range(4):
            gather_copy(n, 0, at, beside).wait_send()

            @pl.when((z < 3) & (at <= z))
            def _():
                gather_copy(n, 1, at, above).wait_send()

            @pl.when((z > 0) & (at >= z))
            def _():
                gather_copy(n, 2, at, below).wait_send()

    sums = ((LP, LY, LU, LD), (IP, IY, IU, ID))

    def pair_copy(n, at):
        P_, Y_, _, _ = sums[n]
        return copy(P_.at[2 * at + 1 - y], Y_.at[at], rs_send.at[n, 0, at], rs_recv.at[n, 0, at], beside)

    def up_copy(n, at):
        P_, _, U_, _ = sums[n]
        return copy(P_.at[2 * at + y], U_.at[at], rs_send.at[n, 1, at], rs_recv.at[n, 1, at], above)

    def down_copy(n, at):
        P_, _, _, D_ = sums[n]
        return copy(P_.at[2 * at + y], D_.at[at], rs_send.at[n, 2, at], rs_recv.at[n, 2, at], below)

    def pair_start(n):
        for d in (3, 2, 1):
            @pl.when(z + d <= 3)
            def _():
                pair_copy(n, z + d).start()

            @pl.when(z - d >= 0)
            def _():
                pair_copy(n, z - d).start()

        pair_copy(n, z).start()

    def sum_line(n):
        P_, Y_, U_, D_ = sums[n]
        for d in (3, 2, 1):
            @pl.when(z + d <= 3)
            def _():
                at = z + d
                pair_copy(n, at).wait_recv()
                P_[2 * at + y] = P_[2 * at + y] + Y_[at]

                @pl.when(z > 0)
                def _():
                    up_copy(n, at).wait_recv()
                    P_[2 * at + y] = P_[2 * at + y] + U_[at]

                up_copy(n, at).start()

            @pl.when(z - d >= 0)
            def _():
                at = z - d
                pair_copy(n, at).wait_recv()
                P_[2 * at + y] = P_[2 * at + y] + Y_[at]

                @pl.when(z < 3)
                def _():
                    down_copy(n, at).wait_recv()
                    P_[2 * at + y] = P_[2 * at + y] + D_[at]

                down_copy(n, at).start()

    def sum_own(n):
        P_, Y_, U_, D_ = sums[n]
        pair_copy(n, z).wait_recv()
        P_[shot] = P_[shot] + Y_[z]

        @pl.when(z > 0)
        def _():
            up_copy(n, z).wait_recv()
            P_[shot] = P_[shot] + U_[z]

        @pl.when(z < 3)
        def _():
            down_copy(n, z).wait_recv()
            P_[shot] = P_[shot] + D_[z]

    def sum_drain(n):
        for at in range(4):
            pair_copy(n, at).wait_send()

            @pl.when(at > z)
            def _():
                up_copy(n, at).wait_send()

            @pl.when(at < z)
            def _():
                down_copy(n, at).wait_send()

    fields = [W.at[0], W.at[1], W.at[2], W.at[3], B.at[0], B.at[1]]

    def halo(n):
        field = fields[n]
        return copy(
            field.at[pl.ds(4 + (nx - 4) * (1 - core), 4), pl.ds(8, ny)],
            field.at[pl.ds((nx + 4) * core, 4), pl.ds(8, ny)],
            halo_send.at[n],
            halo_recv.at[n],
            other,
        )

    gather_start(0)
    load.wait()
    halo(0).start()

    edges = [jnp.full((ny, nz), width_ref[i].astype(jnp.float32)) for i in range(6)]

    def ramp_at(position, count, lower, upper):
        low_part = jnp.maximum(lower - position, 0.0) / lower
        high_part = jnp.maximum(upper - (count - 1.0 - position), 0.0) / upper
        return low_part * low_part + high_part * high_part

    row = lax.broadcasted_iota(jnp.int32, (ny, nz), 0)
    column = lax.broadcasted_iota(jnp.int32, (ny, nz), 1)
    flat = row * nz + column
    BASE[...] = damp_peak * (
        ramp_at(row.astype(jnp.float32), ny, edges[2], edges[3])
        + ramp_at(column.astype(jnp.float32), nz, edges[4], edges[5])
    )

    load_code.wait()

    @pl.loop(0, nx)
    def _(i):
        C[i] = coefficient(CODE[i])
        position = jnp.full((8, nz), (start_x + i).astype(jnp.float32))
        along = ramp_at(position, 2 * nx, edges[0][0:8], edges[1][0:8])
        A[i] = BASE[...] + damp_peak * jnp.concatenate([along] * (ny // 8), axis=0)

    nothing = jnp.zeros((nx, 8, nz), jnp.float32)
    for n in range(6):
        fields[n][pl.ds(4, nx), 0:8, :] = nothing
        fields[n][pl.ds(4, nx), ny + 8 : ny + 16, :] = nothing
        fields[n][pl.ds((nx + 4) * core, 4), 8 : ny + 8, :] = jnp.zeros((4, ny, nz), jnp.float32)

    def along_z(field, i):
        v = field[pl.ds(i + 4, XB), 8 : ny + 8, :].reshape(XB * ny, nz)
        high = v.astype(jnp.bfloat16)
        low = (v - high.astype(jnp.float32)).astype(jnp.bfloat16)
        both = jnp.dot(jnp.concatenate([high, low], axis=1), band_ref[...], preferred_element_type=jnp.float32)
        return both[:, :nz] + both[:, nz:]

    def plane_laplace(field, j, part):
        v = field[j + 4, 8 : ny + 8, :]
        total = 3.0 * STENCIL[0] * v + part
        for k in range(1, 5):
            total = total + STENCIL[k] * (
                (field[j + 4 + k, 8 : ny + 8, :] + field[j + 4 - k, 8 : ny + 8, :])
                + (field[j + 4, 8 + k : ny + 8 + k, :] + field[j + 4, 8 - k : ny + 8 - k, :])
            )
        return v, total

    source = source_ref[0] - start_x * ny * nz

    def wave_step(m):
        halo(m).wait_recv()
        amplitude = wavelet_ref[0, m]

        @pl.loop(0, nx // XB)
        def _(t):
            part = along_z(fields[m], t * XB)
            for p in range(XB):
                j = t * XB + p
                v, total = plane_laplace(fields[m], j, part[p * ny : (p + 1) * ny])
                drive = C[j] * total
                D[m, j] = drive
                if m < 3:
                    prior = PREV[j] if m == 0 else fields[m - 1][j + 4, 8 : ny + 8, :]
                    change = v - prior
                    later = v + change + drive - A[j] * change
                    here = flat == source - j * (ny * nz)
                    later = later + jnp.where(here, C[j] * amplitude, 0.0)
                    fields[m + 1][j + 4, 8 : ny + 8, :] = later

        if m < 3:
            halo(m + 1).start()

    def pack(dest, i, value):
        tiles = swap_groups([value[8 * g : 8 * g + 8] for g in range(groups)], width)
        for g in range(groups):
            dest[g, i] = tiles[g]

    def unpack(n, born, drive):
        @pl.loop(0, nx)
        def _(i):
            tiles = swap_groups([G[n, g, i] for g in range(groups)], width)
            model = jnp.concatenate(tiles, axis=0)
            M[i] = model
            fields[born][i + 4, 8 : ny + 8, :] = model * D[drive, i]

        halo(born).start()

    def born_step(born, drive, finish):
        @pl.loop(0, nx // XB)
        def _(t):
            part = along_z(fields[born], t * XB)
            for p in range(XB):
                j = t * XB + p
                v, total = plane_laplace(fields[born], j, part[p * ny : (p + 1) * ny])
                later = 2.0 * v + C[j] * total - A[j] * v + M[j] * D[drive, j]
                finish(j, v, later)

    gather_forward(0, 1)
    load_prev.wait()
    wave_step(0)
    gather_forward(0, 2)
    wave_step(1)
    gather_forward(0, 3)

    @pl.loop(0, nx)
    def _(i):
        pack(LP, i, D[0, i] * D[0, i] + D[1, i] * D[1, i])

    pair_start(0)
    H[...] = jnp.dot(
        cos_ref[...], gain_ref[...], precision=lax.Precision.HIGHEST, preferred_element_type=jnp.float32
    )
    wave_step(2)
    gather_end(0)
    unpack(0, 4, 0)
    halo(4).wait_recv()

    def finish_image(j, v, later):
        pack(IP, j, D[0, j] * v + D[1, j] * later)

    born_step(4, 1, finish_image)
    pair_start(1)
    sum_line(0)
    wave_step(3)
    sum_line(1)
    sum_own(0)
    sum_own(1)

    sub = lax.broadcasted_iota(jnp.int32, (8, nz), 0)

    @pl.loop(0, nx // 2)
    def _(t):
        for p in range(2):
            i = 2 * t + p
            scaled = IP[shot, i] / (LP[shot, i] + eps)
            moved = [scaled]
            for q in range(1, 8):
                turned = pltpu.roll(scaled, q, 0)
                moved.append(jnp.where(sub < q, pltpu.roll(turned, width, 1), turned))
            result = None
            for g in range(groups):
                term = moved[0] * H[8 * g : 8 * g + 1, :]
                for q in range(1, 8):
                    term = term + moved[q] * H[8 * g + q : 8 * g + q + 1, :]
                if g:
                    result = result + pltpu.roll(term, width * g, 1)
                else:
                    result = term
            G[1, shot, i] = result

    gather_start(1)

    for t in range(nx // groups):
        tiles = swap_groups([G[1, shot, groups * t + g] for g in range(groups)], width)
        turned = jnp.concatenate(tiles, axis=0).T
        filt_ref[groups * t : groups * t + groups] = turned.reshape(groups, width, ny)

    for d in (1, 2, 3):
        gather_forward(1, d)
    gather_end(1)
    unpack(1, 5, 2)

    count = receiver_ref.shape[1]
    lanes = lax.broadcasted_iota(jnp.int32, (1, nz), 1)
    ones = jnp.ones((8, nz), jnp.float32)

    def record(m, read):
        @pl.loop(0, count // 8)
        def _(t):
            for p in range(8):
                r = t * 8 + p
                local = receiver_ref[0, r] - start_x * ny * nz
                owned = (local >= 0) & (local < nx * ny * nz)
                safe = jnp.clip(local, 0, nx * ny * nz - 1)
                at = jnp.where(owned, safe & (nz - 1), -1)
                line = read(safe // (ny * nz), (safe // nz) & (ny - 1))
                ROWS[pl.ds(r, 1), :] = jnp.where(lanes == at, line, 0.0)

        TR[0, m] = lax.dot_general(
            ones, ROWS[...], (((1,), (1,)), ((), ())),
            precision=lax.Precision.HIGHEST, preferred_element_type=jnp.float32,
        )

    halo(5).wait_recv()
    record(0, lambda px, py: B[1, px + 4, pl.ds(py + 8, 1), :])

    def finish_born(j, v, later):
        born_ref[j] = later

    born_step(5, 3, finish_born)
    record(1, lambda px, py: born_ref[px, pl.ds(py, 1), :])
    swap = copy(TR.at[0], TR.at[1], tr_send, tr_recv, other)
    swap.start()
    for n in range(2):
        gather_drain(n)
        sum_drain(n)
    for n in range(6):
        halo(n).wait_send()
    swap.wait()
    for m in range(2):
        trace_ref[m : m + 1, :] = TR[0, m, 0:1, :] + TR[1, m, 0:1, :]


def fast_body(
    wave_prev, wave_now, velocity_code, perturb, gains, wavelet, source_index, receiver_index, absorb_width
):
    shape = wave_now.shape[1:]
    nx, ny, nz = shape
    planes, receivers = gains.shape[0], receiver_index.shape[1]
    groups = nz // planes
    index = np.arange(ny)
    cosine = (np.cos(2.0 * np.pi / ny * (index[:, None] * index[None, :] % ny)) / ny).astype(np.float32)
    band = np.zeros((nz, nz), np.float32)
    for k in range(1, 5):
        band += STENCIL[k] * (np.eye(nz, k=k) + np.eye(nz, k=-k)).astype(np.float32)
    high = band.astype(ml_dtypes.bfloat16)
    low = (band - high.astype(np.float32)).astype(ml_dtypes.bfloat16)
    band = np.concatenate([np.concatenate([high, low], 1)] * 2, 0)
    tiled = jnp.tile(gains.T, (1, groups))
    block = (nx, 8, nz)
    f32 = jnp.float32
    vmem = pl.BlockSpec(memory_space=pltpu.VMEM)
    smem = pl.BlockSpec(memory_space=pltpu.SMEM)
    v = lambda *dims: pltpu.VMEM(dims, f32)
    dma = pltpu.SemaphoreType.DMA
    filtered, born, traces = pl.pallas_call(
        window_kernel,
        out_shape=(
            jax.ShapeDtypeStruct((nx, planes, ny), f32),
            jax.ShapeDtypeStruct(shape, f32),
            jax.ShapeDtypeStruct((STEPS_B, receivers), f32),
        ),
        in_specs=[pl.BlockSpec(memory_space=pl.ANY)] * 3 + [vmem] * 4 + [smem] * 4,
        out_specs=(vmem, vmem, vmem),
        scratch_shapes=[
            v(4, nx + 8, ny + 16, nz),
            v(4, *shape),
            v(2, nx + 8, ny + 16, nz),
            v(*shape),
            v(*shape),
            v(*shape),
            pltpu.VMEM(shape, jnp.int32),
            v(*shape),
            v(ny, nz),
            v(2, groups, *block),
        ]
        + [v(groups, *block), v(4, *block), v(4, *block), v(4, *block)] * 2
        + [
            v(ny, nz),
            v(receivers, nz),
            v(2, STEPS_B, 8, receivers),
            dma,
            dma,
            dma,
            dma((6,)),
            dma((6,)),
            dma,
            dma,
            dma((2, 3, 4)),
            dma((2, groups)),
            dma((2, 3, 4)),
            dma((2, 3, 4)),
        ],
        compiler_params=pltpu.CompilerParams(
            collective_id=0, has_side_effects=True, vmem_limit_bytes=60 * 1024 * 1024
        ),
    )(
        wave_prev.reshape(shape), wave_now.reshape(shape), velocity_code, perturb.transpose(0, 2, 1), tiled, cosine, band,
        wavelet, source_index, receiver_index, absorb_width,
    )
    return filtered.transpose(0, 2, 1), born[None], traces[None]


def choose(*args):
    wave_now, gains = args[1], args[4]
    shots, _, span_y, span_z = wave_now.shape
    size = lax.axis_size("shot")
    fits = shots == 1 and size == 8 and lax.axis_size("space") == 2
    if fits and span_y == 64 and span_z == 128 and gains.shape[0] == 16:
        return fast_body(*args)
    return body(*args)


def solution(mesh):
    in_specs = (
        P(("dom", "shot"), "space", None, None),
        P(("dom", "shot"), "space", None, None),
        P(("dom", "space"), None, None),
        P(("dom", "space"), None, "shot"),
        P(("dom", "shot"), None),
        P(("dom", "shot"), None),
        P(("dom", "shot")),
        P(("dom", "shot"), None),
        P("dom"),
    )
    out_specs = (
        P(("dom", "space"), None, "shot"),
        P(("dom", "shot"), "space", None, None),
        P(("dom", "shot"), None, None),
    )
    return jax.shard_map(choose, mesh=mesh, in_specs=in_specs, out_specs=out_specs, check_vma=False)
```
